32 devices in a mesh: groups: 2 (over y), gx: 4 (over z), gy: 2 (over x), gz: 2 (over core).
Axes of the slice: x: 2, y: 2, z: 4, core: 2. Of those that a mesh axis runs over, the one named last changes fastest.
Arguments:
- activations: bfloat16 [3072, 8192], P(('groups', 'gz', 'gx'), 'gy'), parts along dimension 0, may hold values from -0.29882812 to 0.29882812
- gate_pre: bfloat16 [3072, 14336], P(('groups', 'gz', 'gy'), 'gx'), parts along dimension 0, may hold values from -6 to 6
- up_pre: bfloat16 [3072, 14336], P(('groups', 'gz', 'gy'), 'gx'), parts along dimension 0, may hold values from -6 to 6
- gate_weight: bfloat16 [8192, 14336], P(('gy', 'gz'), 'gx'), may hold values from -0.0625 to 0.0625
- up_weight: bfloat16 [8192, 14336], P(('gy', 'gz'), 'gx'), may hold values from -0.0625 to 0.0625
- down_weight: bfloat16 [14336, 8192], P(('gx', 'gz'), 'gy'), may hold values from -0.046875 to 0.046875
- out_grad: bfloat16 [3072, 8192], P(('groups', 'gz', 'gx'), 'gy'), parts along dimension 0, may hold values from -6 to 6
Outputs:
- input_grad: bfloat16 [3072, 8192], P(('groups', 'gz', 'gx'), 'gy'), parts along dimension 0
- gate_wgrad: bfloat16 [16384, 14336], P(('groups', 'gy', 'gz'), 'gx'), parts along dimension 0
- up_wgrad: bfloat16 [16384, 14336], P(('groups', 'gy', 'gz'), 'gx'), parts along dimension 0
The draws below stay inside these ranges and needn't reach their ends.
There are 2 independent parts, one for each index of `groups`. The reference program is written for one: setup_inputs(seed, part) draws one part's arguments, and reference() takes and returns one part's arrays. A program takes and returns all parts, laid end to end along the dimension named above; an argument that names none is the same for every part. Nothing has to cross between parts.
All inputs are finite; a program needn't handle non-finite values.
Results may differ from the reference program's by a relative error of at most 0.015.
Values may be sent and summed in bfloat16 or wider, within the bound.
A program may use at most 384 MiB of HBM per device.

```python
import jax
import jax.numpy as jnp

D = 8192
FF = 14336
TOKENS = 1536
N_GX = 4
N_GY = 2


def level_of(key, dims, cuts, least, largest):
    level = 1.0
    for position, shards_of in cuts:
        steps = jax.random.uniform(jax.random.fold_in(jax.random.fold_in(key, 6), position), (shards_of,), jnp.float32, least / len(cuts), largest / len(cuts))
        level = level * jnp.repeat(jnp.exp(steps), dims[position] // shards_of).reshape((-1,) + (1,) * (len(dims) - 1 - position))
    return level


def bell_draw(key, dims, spread, reach, split=(), held_as=jnp.bfloat16):
    array = spread * jax.random.normal(key, dims, jnp.float32)
    if split:
        array = array * level_of(key, dims, split, -0.22, 0.18)
    return jnp.clip(array, -reach, reach).astype(held_as)


def setup_inputs(seed: int = 0, part: int = 0) -> dict:
    seeds = jax.random.split(jax.random.key(seed), 8)
    part_splits = jax.random.split(jax.random.fold_in(seeds[7], part), 8)
    return {
        "activations": bell_draw(part_splits[0], (TOKENS, D), 0.05, 0.29882812, ((0, 8), (1, 2))),
        "gate_pre": bell_draw(part_splits[1], (TOKENS, FF), 1.0, 6.0, ((0, 4), (1, 4))),
        "up_pre": bell_draw(part_splits[2], (TOKENS, FF), 1.0, 6.0, ((0, 4), (1, 4))),
        "gate_weight": bell_draw(seeds[3], (D, FF), D ** -0.5, 0.0625, ((0, 4), (1, 4))),
        "up_weight": bell_draw(seeds[4], (D, FF), D ** -0.5, 0.0625, ((0, 4), (1, 4))),
        "down_weight": bell_draw(seeds[5], (FF, D), FF ** -0.5, 0.046875, ((0, 8), (1, 2))),
        "out_grad": bell_draw(part_splits[6], (TOKENS, D), 1.0, 6.0, ((0, 8), (1, 2))),
    }


def silu_backward(hidden_grad, gate_pre, up_pre):
    gate_value = gate_pre.astype(jnp.float32)
    up_value = up_pre.astype(jnp.float32)
    sigmoid_gate = jax.nn.sigmoid(gate_value)
    gate_grad = (hidden_grad * up_value * sigmoid_gate * (1.0 + gate_value * (1.0 - sigmoid_gate))).astype(jnp.bfloat16)
    up_grad = (hidden_grad * gate_value * sigmoid_gate).astype(jnp.bfloat16)
    return gate_grad, up_grad


def reference(activations, gate_pre, up_pre, gate_weight, up_weight, down_weight, out_grad):
    feat_block = D // N_GY
    hidden_grad = jnp.zeros((out_grad.shape[0], FF), jnp.float32)
    for block in range(N_GY):
        cols = slice(block * feat_block, (block + 1) * feat_block)
        part = jnp.dot(out_grad[:, cols], down_weight[:, cols].T, preferred_element_type=jnp.float32)
        hidden_grad = hidden_grad + part.astype(jnp.bfloat16).astype(jnp.float32)
    gate_grad, up_grad = silu_backward(hidden_grad, gate_pre, up_pre)
    unit_block = FF // N_GX
    input_grad = jnp.zeros((out_grad.shape[0], D), jnp.float32)
    for block in range(N_GX):
        cols = slice(block * unit_block, (block + 1) * unit_block)
        part = jnp.dot(gate_grad[:, cols], gate_weight[:, cols].T, preferred_element_type=jnp.float32)
        part = part + jnp.dot(up_grad[:, cols], up_weight[:, cols].T, preferred_element_type=jnp.float32)
        input_grad = input_grad + part.astype(jnp.bfloat16).astype(jnp.float32)
    gate_wgrad = jnp.dot(activations.T, gate_grad, preferred_element_type=jnp.float32)
    up_wgrad = jnp.dot(activations.T, up_grad, preferred_element_type=jnp.float32)
    return input_grad.astype(jnp.bfloat16), gate_wgrad.astype(jnp.bfloat16), up_wgrad.astype(jnp.bfloat16)
```

```python
import jax
import jax.numpy as jnp
from jax import lax
from jax.sharding import PartitionSpec as P


def silu_backward(hidden_grad, gate_pre, up_pre):
    gate_value = gate_pre.astype(jnp.float32)
    up_value = up_pre.astype(jnp.float32)
    sigmoid_gate = jax.nn.sigmoid(gate_value)
    gate_grad = (
        hidden_grad * up_value * sigmoid_gate * (1.0 + gate_value * (1.0 - sigmoid_gate))
    ).astype(jnp.bfloat16)
    up_grad = (hidden_grad * gate_value * sigmoid_gate).astype(jnp.bfloat16)
    return (gate_grad, up_grad)


def times_transpose(left, right):
    return lax.dot_general(
        left, right, (((1,), (1,)), ((), ())), preferred_element_type=jnp.float32
    )


def pick(index, choices):
    result = choices[-1]
    for place in range(len(choices) - 2, -1, -1):
        if choices[place] is not choices[place + 1]:
            result = jnp.where(index <= place, choices[place], result)
    return result


def pick_number(index, numbers):
    result = jnp.int32(numbers[-1])
    for place in range(len(numbers) - 2, -1, -1):
        result = jnp.where(index == place, jnp.int32(numbers[place]), result)
    return result


def slot_table(size):
    return [sorted(range(size), key=lambda block: (abs(block - place), block)) for place in range(size)]


def line_steps(size):
    to_right = [(place, place + 1) for place in range(size - 1)]
    to_left = [(place + 1, place) for place in range(size - 1)]
    return to_right, to_left


def tie(*arrays):
    return lax.optimization_barrier(arrays)


def slot_of(slot, rightward, leftward, axis, size):
    table = slot_table(size)
    choices = []
    for at in range(size):
        source = table[at][slot]
        choices.append(rightward[at - source] if source < at else leftward[source - at])
    return pick(lax.axis_index(axis), choices)


def cut_rows(rows, pieces):
    cuts = sorted({rows * piece // pieces // 16 * 16 for piece in range(pieces)} | {rows})
    return list(zip(cuts[:-1], cuts[1:]))


def line_reduce_scatter(parts, axis, size, beside):
    table = slot_table(size)
    place = lax.axis_index(axis)
    to_right = [(at, at + 1) for at in range(size - 1)]
    to_left = [(at + 1, at) for at in range(size - 1)]

    def part_for(offset):
        choices, last = [None] * size, None
        for at in range(size):
            if 0 <= at + offset < size:
                choices[at] = parts[table[at].index(at + offset)]
        known = [choice for choice in choices if choice is not None]
        last = known[0]
        for at in range(size):
            last = choices[at] if choices[at] is not None else last
            choices[at] = last
        return pick(place, choices)

    right_sum = left_sum = None
    parts = list(parts)
    for distance in range(size - 1, 0, -1):
        right_part, left_part = part_for(distance), part_for(-distance)
        if right_sum is not None:
            right_part = (right_part.astype(jnp.float32) + right_sum.astype(jnp.float32)).astype(jnp.bfloat16)
            left_part = (left_part.astype(jnp.float32) + left_sum.astype(jnp.float32)).astype(jnp.bfloat16)
        right_sum = lax.ppermute(right_part, axis, to_right)
        left_sum = lax.ppermute(left_part, axis, to_left)
        if distance == size - 1 and distance > 1:
            right_sum, left_sum, parts[0] = tie(right_sum, left_sum, parts[0])
        elif distance == 2:
            right_sum, left_sum, beside = tie(right_sum, left_sum, beside)
    own = parts[0].astype(jnp.float32)
    if right_sum is not None:
        own = own + right_sum.astype(jnp.float32) + left_sum.astype(jnp.float32)
    return own.astype(jnp.bfloat16), beside


def shifted(array, axis, size, shift):
    return lax.ppermute(array, axis, [(place, (place + shift) % size) for place in range(size)])


def make_on_device(mesh):
    n_gx, n_gy, n_gz = mesh.shape["gx"], mesh.shape["gy"], mesh.shape["gz"]
    table = slot_table(n_gx)

    def on_device(activations, gate_pre, up_pre, gate_weight, up_weight, down_weight, out_grad):
        rows = out_grad.shape[0]
        z = lax.axis_index("gx")
        core = lax.axis_index("gz")
        down_block = lax.all_gather(down_weight, "gz", axis=0, tiled=True)
        gate_block = lax.all_gather(gate_weight, "gz", axis=0, tiled=True)
        up_block = lax.all_gather(up_weight, "gz", axis=0, tiled=True)
        to_right, to_left = line_steps(n_gx)

        width = activations.shape[1] // n_gz
        own_half = lax.dynamic_slice(activations, (0, core * width), (rows, width))
        act_rows = [own_half]
        for shift in range(1, n_gz):
            theirs = lax.dynamic_slice(
                activations, (0, ((core - shift) % n_gz) * width), (rows, width)
            )
            act_rows.append(shifted(theirs, "gz", n_gz, -shift))
        act_block = jnp.concatenate(act_rows, axis=0)

        y = lax.axis_index("gy")

        groups = [list(range(first, min(first + 2, n_gx))) for first in range(0, n_gx, 2)]
        own_rows, units = gate_pre.shape
        gate_slab = jnp.zeros((own_rows * n_gy, units), gate_pre.dtype)
        gate_slab = lax.dynamic_update_slice(gate_slab, gate_pre, (y * own_rows, 0))
        up_slab = jnp.zeros((own_rows * n_gy, units), up_pre.dtype)
        up_slab = lax.dynamic_update_slice(up_slab, up_pre, (y * own_rows, 0))
        steps = max(n_gx - 1, 1)
        cuts = cut_rows(own_rows, steps)
        rightward, leftward, cotangents = [out_grad], [out_grad], [out_grad]
        parts = [None] * len(groups)
        right, left = out_grad, out_grad
        pieces_left = [(gate_pre[low:high], up_pre[low:high]) for low, high in cuts]
        arrivals = []
        for step in range(1, steps + 1):
            if n_gx > 1:
                right, left = lax.ppermute(right, "gx", to_right), lax.ppermute(left, "gx", to_left)
            beside = []
            if step <= len(cuts):
                for piece in pieces_left[step - 1]:
                    beside.append(
                        [shifted(piece, "gy", n_gy, shift) for shift in range(1, n_gy)]
                    )
            right, left, beside, pieces_left, parts = lax.optimization_barrier(
                (right, left, beside, pieces_left, parts)
            )
            if beside:
                arrivals.append(beside)
            if n_gx > 1:
                rightward.append(right)
                leftward.append(left)
                cotangents.append(slot_of(step, rightward, leftward, "gx", n_gx))
            for index, group in enumerate(groups):
                if group[-1] == step or (step == steps and parts[index] is None):
                    parts[index] = times_transpose(
                        jnp.concatenate([cotangents[slot] for slot in group], axis=0), down_block
                    ).astype(jnp.bfloat16)
        for (low, _), (gate_arrived, up_arrived) in zip(cuts, arrivals):
            for shift in range(1, n_gy):
                first = ((y - shift) % n_gy) * own_rows + low
                gate_slab = lax.dynamic_update_slice(gate_slab, gate_arrived[shift - 1], (first, 0))
                up_slab = lax.dynamic_update_slice(up_slab, up_arrived[shift - 1], (first, 0))

        waiting = []
        for group, part in zip(groups, parts):
            waiting += [part[k * rows : (k + 1) * rows] for k in range(len(group))]
        act_block, right = tie(act_block, right)
        rightward, leftward, act_slots = [act_block], [act_block], [act_block]
        right, left = act_block, act_block
        hidden = [None] * n_gx
        order = [0] + list(range(n_gx - 1, 0, -1))
        for step, slot in enumerate(order, 1):
            arrived = [shifted(waiting[slot], "gy", n_gy, shift) for shift in range(1, n_gy)]
            if step < n_gx:
                right, left = lax.ppermute(right, "gx", to_right), lax.ppermute(left, "gx", to_left)
                right, left, arrived, waiting = lax.optimization_barrier(
                    (right, left, arrived, waiting)
                )
                rightward.append(right)
                leftward.append(left)
                act_slots.append(slot_of(step, rightward, leftward, "gx", n_gx))
            hidden[slot] = [waiting[slot]] + arrived

        gate_pieces, up_pieces, act_pieces, input_parts = [], [], [], [None] * n_gx
        for index, group in reversed(list(enumerate(groups))):
            sums, gates, ups = [], [], []
            for slot in group:
                total = hidden[slot][0].astype(jnp.float32)
                for other in hidden[slot][1:]:
                    total = total + other.astype(jnp.float32)
                first = pick_number(z, [table[at][slot] for at in range(n_gx)]) * rows
                sums.append(total)
                gates.append(lax.dynamic_slice(gate_slab, (first, 0), (rows, units)))
                ups.append(lax.dynamic_slice(up_slab, (first, 0), (rows, units)))
            pairs = [silu_backward(*three) for three in zip(sums, gates, ups)]
            gate_grad = jnp.concatenate([pair[0] for pair in pairs], axis=0)
            up_grad = jnp.concatenate([pair[1] for pair in pairs], axis=0)
            input_part = (
                times_transpose(gate_grad, gate_block) + times_transpose(up_grad, up_block)
            ).astype(jnp.bfloat16)
            if index == 1:
                input_part, hidden[order[-1]] = tie(input_part, hidden[order[-1]])
            for place, slot in enumerate(group):
                input_parts[slot] = input_part[place * rows : (place + 1) * rows]
            for grad, pieces in ((gate_grad, gate_pieces), (up_grad, up_pieces)):
                pieces += [grad] + [shifted(grad, "gz", n_gz, shift) for shift in range(1, n_gz)]
            for shift in range(n_gz):
                act_pieces += [
                    act_slots[slot][shift * rows : (shift + 1) * rows] for slot in group
                ]
        act_every = lax.optimization_barrier(jnp.concatenate(act_pieces, axis=0).T)
        gate_every = jnp.concatenate(gate_pieces, axis=0)
        up_every = jnp.concatenate(up_pieces, axis=0)
        gate_wgrad = jnp.dot(act_every, gate_every, preferred_element_type=jnp.float32)
        input_grad, gate_wgrad = line_reduce_scatter(
            input_parts, "gx", n_gx, gate_wgrad.astype(jnp.bfloat16)
        )
        up_wgrad = jnp.dot(act_every, up_every, preferred_element_type=jnp.float32)
        return (input_grad, gate_wgrad, up_wgrad.astype(jnp.bfloat16))

    return on_device


def solution(mesh):
    return jax.shard_map(
        make_on_device(mesh),
        mesh=mesh,
        in_specs=(
            P(("groups", "gz", "gx"), "gy"),
            P(("groups", "gz", "gy"), "gx"),
            P(("groups", "gz", "gy"), "gx"),
            P(("gy", "gz"), "gx"),
            P(("gy", "gz"), "gx"),
            P(("gx", "gz"), "gy"),
            P(("groups", "gz", "gx"), "gy"),
        ),
        out_specs=(
            P(("groups", "gz", "gx"), "gy"),
            P(("groups", "gy", "gz"), "gx"),
            P(("groups", "gy", "gz"), "gx"),
        ),
        check_vma=False,
    )
```

```python
import jax
import jax.numpy as jnp
from jax import lax
from jax.sharding import PartitionSpec as P


def silu_backward(hidden_grad, gate_pre, up_pre):
    gate_value = gate_pre.astype(jnp.float32)
    up_value = up_pre.astype(jnp.float32)
    sigmoid_gate = jax.nn.sigmoid(gate_value)
    gate_grad = (
        hidden_grad * up_value * sigmoid_gate * (1.0 + gate_value * (1.0 - sigmoid_gate))
    ).astype(jnp.bfloat16)
    up_grad = (hidden_grad * gate_value * sigmoid_gate).astype(jnp.bfloat16)
    return (gate_grad, up_grad)


def times_transpose(left, right):
    return lax.dot_general(
        left, right, (((1,), (1,)), ((), ())), preferred_element_type=jnp.float32
    )


def pick(index, choices):
    result = choices[-1]
    for place in range(len(choices) - 2, -1, -1):
        if choices[place] is not choices[place + 1]:
            result = jnp.where(index <= place, choices[place], result)
    return result


def pick_number(index, numbers):
    result = jnp.int32(numbers[-1])
    for place in range(len(numbers) - 2, -1, -1):
        result = jnp.where(index == place, jnp.int32(numbers[place]), result)
    return result


def slot_table(size):
    return [sorted(range(size), key=lambda block: (abs(block - place), block)) for place in range(size)]


def line_steps(size):
    to_right = [(place, place + 1) for place in range(size - 1)]
    to_left = [(place + 1, place) for place in range(size - 1)]
    return to_right, to_left


def tie(*arrays):
    return lax.optimization_barrier(arrays)


def slot_of(slot, rightward, leftward, axis, size):
    table = slot_table(size)
    choices = []
    for at in range(size):
        source = table[at][slot]
        choices.append(rightward[at - source] if source < at else leftward[source - at])
    return pick(lax.axis_index(axis), choices)


def cut_rows(rows, pieces):
    cuts = sorted({rows * piece // pieces // 16 * 16 for piece in range(pieces)} | {rows})
    return list(zip(cuts[:-1], cuts[1:]))


def line_reduce_scatter(parts, axis, size, beside):
    table = slot_table(size)
    place = lax.axis_index(axis)
    to_right = [(at, at + 1) for at in range(size - 1)]
    to_left = [(at + 1, at) for at in range(size - 1)]

    def part_for(offset):
        choices, last = [None] * size, None
        for at in range(size):
            if 0 <= at + offset < size:
                choices[at] = parts[table[at].index(at + offset)]
        known = [choice for choice in choices if choice is not None]
        last = known[0]
        for at in range(size):
            last = choices[at] if choices[at] is not None else last
            choices[at] = last
        return pick(place, choices)

    right_sum = left_sum = None
    beside = list(beside)
    for distance in range(size - 1, 0, -1):
        right_part, left_part = part_for(distance), part_for(-distance)
        if right_sum is not None:
            right_part = (right_part.astype(jnp.float32) + right_sum.astype(jnp.float32)).astype(jnp.bfloat16)
            left_part = (left_part.astype(jnp.float32) + left_sum.astype(jnp.float32)).astype(jnp.bfloat16)
        right_sum = lax.ppermute(right_part, axis, to_right)
        left_sum = lax.ppermute(left_part, axis, to_left)
        if size - 1 - distance < len(beside):
            index = size - 1 - distance
            right_sum, left_sum, beside[index] = tie(right_sum, left_sum, beside[index])
    own = parts[0].astype(jnp.float32)
    if right_sum is not None:
        own = own + right_sum.astype(jnp.float32) + left_sum.astype(jnp.float32)
    return own.astype(jnp.bfloat16), beside


def shifted(array, axis, size, shift):
    return lax.ppermute(array, axis, [(place, (place + shift) % size) for place in range(size)])


def make_on_device(mesh):
    n_gx, n_gy, n_gz = mesh.shape["gx"], mesh.shape["gy"], mesh.shape["gz"]
    table = slot_table(n_gx)

    def on_device(activations, gate_pre, up_pre, gate_weight, up_weight, down_weight, out_grad):
        rows = out_grad.shape[0]
        z = lax.axis_index("gx")
        core = lax.axis_index("gz")
        down_block = lax.all_gather(down_weight, "gz", axis=0, tiled=True)
        gate_block = lax.all_gather(gate_weight, "gz", axis=0, tiled=True)
        up_block = lax.all_gather(up_weight, "gz", axis=0, tiled=True)
        to_right, to_left = line_steps(n_gx)

        width = activations.shape[1] // n_gz
        own_half = lax.dynamic_slice(activations, (0, core * width), (rows, width))
        act_rows = [own_half]
        for shift in range(1, n_gz):
            theirs = lax.dynamic_slice(
                activations, (0, ((core - shift) % n_gz) * width), (rows, width)
            )
            act_rows.append(shifted(theirs, "gz", n_gz, -shift))
        act_block = jnp.concatenate(act_rows, axis=0)

        y = lax.axis_index("gy")

        groups = [list(range(first, min(first + 2, n_gx))) for first in range(0, n_gx, 2)]
        own_rows, units = gate_pre.shape
        gate_slab = jnp.zeros((own_rows * n_gy, units), gate_pre.dtype)
        gate_slab = lax.dynamic_update_slice(gate_slab, gate_pre, (y * own_rows, 0))
        up_slab = jnp.zeros((own_rows * n_gy, units), up_pre.dtype)
        up_slab = lax.dynamic_update_slice(up_slab, up_pre, (y * own_rows, 0))
        steps = max(n_gx - 1, 1)
        cuts = cut_rows(own_rows, steps)
        rightward, leftward, cotangents = [out_grad], [out_grad], [out_grad]
        parts = [None] * len(groups)
        right, left = out_grad, out_grad
        pieces_left = [(gate_pre[low:high], up_pre[low:high]) for low, high in cuts]
        arrivals = []
        for step in range(1, steps + 1):
            if n_gx > 1:
                right, left = lax.ppermute(right, "gx", to_right), lax.ppermute(left, "gx", to_left)
            beside = []
            if step <= len(cuts):
                for piece in pieces_left[step - 1]:
                    beside.append(
                        [shifted(piece, "gy", n_gy, shift) for shift in range(1, n_gy)]
                    )
            right, left, beside, pieces_left, parts = lax.optimization_barrier(
                (right, left, beside, pieces_left, parts)
            )
            if beside:
                arrivals.append(beside)
            if n_gx > 1:
                rightward.append(right)
                leftward.append(left)
                cotangents.append(slot_of(step, rightward, leftward, "gx", n_gx))
            for index, group in enumerate(groups):
                if group[-1] == step or (step == steps and parts[index] is None):
                    parts[index] = times_transpose(
                        jnp.concatenate([cotangents[slot] for slot in group], axis=0), down_block
                    ).astype(jnp.bfloat16)
        for (low, _), (gate_arrived, up_arrived) in zip(cuts, arrivals):
            for shift in range(1, n_gy):
                first = ((y - shift) % n_gy) * own_rows + low
                gate_slab = lax.dynamic_update_slice(gate_slab, gate_arrived[shift - 1], (first, 0))
                up_slab = lax.dynamic_update_slice(up_slab, up_arrived[shift - 1], (first, 0))

        waiting = []
        for group, part in zip(groups, parts):
            waiting += [part[k * rows : (k + 1) * rows] for k in range(len(group))]
        act_block, right = tie(act_block, right)
        rightward, leftward, act_slots = [act_block], [act_block], [act_block]
        right, left = act_block, act_block
        hidden = [None] * n_gx
        order = groups[0] + list(range(n_gx - 1, len(groups[0]) - 1, -1))
        for step, slot in enumerate(order, 1):
            arrived = [shifted(waiting[slot], "gy", n_gy, shift) for shift in range(1, n_gy)]
            if step < n_gx:
                right, left = lax.ppermute(right, "gx", to_right), lax.ppermute(left, "gx", to_left)
                right, left, arrived, waiting = lax.optimization_barrier(
                    (right, left, arrived, waiting)
                )
                rightward.append(right)
                leftward.append(left)
                act_slots.append(slot_of(step, rightward, leftward, "gx", n_gx))
            hidden[slot] = [waiting[slot]] + arrived

        gate_pieces, up_pieces, act_pieces, input_parts = [], [], [], [None] * n_gx
        turns = [0] + list(range(len(groups) - 1, 0, -1))
        for index, group in [(turn, groups[turn]) for turn in turns]:
            sums, gates, ups = [], [], []
            for slot in group:
                total = hidden[slot][0].astype(jnp.float32)
                for other in hidden[slot][1:]:
                    total = total + other.astype(jnp.float32)
                first = pick_number(z, [table[at][slot] for at in range(n_gx)]) * rows
                sums.append(total)
                gates.append(lax.dynamic_slice(gate_slab, (first, 0), (rows, units)))
                ups.append(lax.dynamic_slice(up_slab, (first, 0), (rows, units)))
            pairs = [silu_backward(*three) for three in zip(sums, gates, ups)]
            gate_grad = jnp.concatenate([pair[0] for pair in pairs], axis=0)
            up_grad = jnp.concatenate([pair[1] for pair in pairs], axis=0)
            input_part = (
                times_transpose(gate_grad, gate_block) + times_transpose(up_grad, up_block)
            ).astype(jnp.bfloat16)
            if index == 0 and len(groups) > 1:
                input_part, hidden[order[-1]] = tie(input_part, hidden[order[-1]])
            for place, slot in enumerate(group):
                input_parts[slot] = input_part[place * rows : (place + 1) * rows]
            for grad, pieces in ((gate_grad, gate_pieces), (up_grad, up_pieces)):
                pieces += [grad] + [shifted(grad, "gz", n_gz, shift) for shift in range(1, n_gz)]
            for shift in range(n_gz):
                act_pieces += [
                    act_slots[slot][shift * rows : (shift + 1) * rows] for slot in group
                ]
        act_every = lax.optimization_barrier(jnp.concatenate(act_pieces, axis=0).T)
        gate_every = jnp.concatenate(gate_pieces, axis=0)
        up_every = jnp.concatenate(up_pieces, axis=0)
        gate_wgrad = jnp.dot(act_every, gate_every, preferred_element_type=jnp.float32)
        up_wgrad = jnp.dot(act_every, up_every, preferred_element_type=jnp.float32)
        input_grad, wgrads = line_reduce_scatter(
            input_parts, "gx", n_gx, [gate_wgrad.astype(jnp.bfloat16), up_wgrad.astype(jnp.bfloat16)]
        )
        return (input_grad, *wgrads)

    return on_device


def solution(mesh):
    return jax.shard_map(
        make_on_device(mesh),
        mesh=mesh,
        in_specs=(
            P(("groups", "gz", "gx"), "gy"),
            P(("groups", "gz", "gy"), "gx"),
            P(("groups", "gz", "gy"), "gx"),
            P(("gy", "gz"), "gx"),
            P(("gy", "gz"), "gx"),
            P(("gx", "gz"), "gy"),
            P(("groups", "gz", "gx"), "gy"),
        ),
        out_specs=(
            P(("groups", "gz", "gx"), "gy"),
            P(("groups", "gy", "gz"), "gx"),
            P(("groups", "gy", "gz"), "gx"),
        ),
        check_vma=False,
    )
```
